512 devices in a mesh: dp: 64 (over x, z), mp: 8 (over y, core).
Axes of the slice: x: 4, y: 4, z: 16, core: 2. Of those that a mesh axis runs over, the one named last changes fastest.
Arguments:
- latent_in: bfloat16 [64, 34, 32, 1280], P('dp', None, None, 'mp'), may hold values from -6 to 6
- out_grad: bfloat16 [64, 32, 32, 1280], P('dp'), may hold values from -2.5 to 2.5
- q_prev: bfloat16 [9, 1280, 64], P(None, 'mp'), may hold values from -6 to 6
Outputs:
- p_factor: float32 [1280, 64], P('dp')
- q_factor: float32 [9, 1280, 64], P(None, 'mp')
The draws below stay inside these ranges and needn't reach their ends.
All inputs are finite; a program needn't handle non-finite values.
Results may differ from the reference program's by a relative error of at most 0.0003.
Values sent between devices are 32-bit elements; how exact they have to be, the bound alone decides.
No kernel may reach another device: no remote copies, remote signals or barrier semaphores. Data moves between devices by JAX's collectives and lax.ppermute only.
A program may use at most 64 MiB of HBM per device.

```python
import math
import jax
import jax.numpy as jnp
from jax import lax

CIN = 1280
COUT = 1280
RANK = 64
TAPS = 9
WIDTH = 32
ROWS = 32
SAMPLES = 64
N_DP = 64


def strengthened(array, own_key, source, target, blocks, factor):
    def block_of(position):
        return (jnp.arange(array.shape[position]) // (array.shape[position] // blocks)).reshape((-1,) + (1,) * (array.ndim - 1 - position))

    first = jax.random.permutation(own_key, blocks)[block_of(target)]
    other_side = (block_of(target) + blocks // 2) % blocks
    return jnp.where((block_of(source) == first) | (block_of(source) == other_side), factor * array, array)


def levels(rng, dims, shards, smallest, largest):
    factor_of, own = 1.0, jax.random.fold_in(rng, 6)
    for position, blocks in shards:
        draws = jnp.exp(jax.random.uniform(jax.random.fold_in(own, position), (blocks,), jnp.float32, smallest / len(shards), largest / len(shards)))
        factor_of = factor_of * jnp.repeat(draws, dims[position] // blocks).reshape([-1 if axis == position else 1 for axis in range(len(dims))])
    return factor_of


def scatter_about(own_key, shape, width, bound, cuts=(), kind=jnp.bfloat16):
    array = width * jax.random.normal(own_key, shape, jnp.float32)
    if cuts:
        array = array * levels(own_key, shape, cuts, -0.22, 0.18)
    return jnp.clip(array, -bound, bound).astype(kind)


def heavy_noise(own_key, extent, scale, bound, split, heavy, kind=jnp.bfloat16):
    array = scale * jax.random.normal(own_key, extent, jnp.float32)
    if split:
        array = array * levels(own_key, extent, split, -0.22, 0.18)
    return jnp.clip(strengthened(array, jax.random.fold_in(own_key, 3), *heavy), -bound, bound).astype(kind)


def setup_inputs(seed: int = 0) -> dict:
    splits = jax.random.split(jax.random.key(seed), 4)
    return {
        "latent_in": scatter_about(splits[0], (SAMPLES, ROWS + 2, WIDTH, CIN), 1.0, 6.0, ((0, 64), (3, 8))),
        "out_grad": heavy_noise(splits[1], (SAMPLES, ROWS, WIDTH, COUT), (max(ROWS * WIDTH * N_DP // 1296, 1)) ** -0.5, 2.5, ((0, 64),), (0, 3, 64, 4.0)),
        "q_prev": scatter_about(splits[2], (TAPS, CIN, RANK), 1.0, 6.0, ((1, 8),)),
    }


def columns_of(sample_x):
    padded = jnp.pad(sample_x, ((0, 0), (1, 1), (0, 0)))
    pieces = [padded[tap_row:tap_row + ROWS, tap_col:tap_col + WIDTH, :].reshape(ROWS * WIDTH, CIN) for tap_row in range(3) for tap_col in range(3)]
    return jnp.concatenate(pieces, axis=1)

def reference(latent_in, out_grad, q_prev):
    q_flat = q_prev.reshape(TAPS * CIN, RANK)

    def p_step(running, sample_pair):
        sample_x, sample_g = sample_pair
        projected = jnp.dot(columns_of(sample_x).astype(jnp.float32), q_flat.astype(jnp.float32), preferred_element_type=jnp.float32)
        grads = sample_g.reshape(ROWS * WIDTH, COUT).astype(jnp.float32)
        return (running + jnp.dot(grads.T, projected, precision=lax.Precision.HIGHEST), None)
    p_sum, unused = lax.scan(p_step, jnp.zeros((COUT, RANK), jnp.float32), (latent_in, out_grad))
    gram_matrix = jnp.dot(p_sum.T, p_sum, precision=lax.Precision.HIGHEST)
    factor_low = jnp.linalg.cholesky(gram_matrix)
    solved = lax.linalg.triangular_solve(factor_low, p_sum.T, left_side=True, lower=True)
    p_factor = math.sqrt(COUT) * solved.T

    def q_step(running, sample_pair):
        sample_x, sample_g = sample_pair
        grads = sample_g.reshape(ROWS * WIDTH, COUT).astype(jnp.float32)
        mapped = jnp.dot(grads, p_factor, precision=lax.Precision.HIGHEST)
        wide_cols = columns_of(sample_x).astype(jnp.float32)
        return (running + jnp.dot(wide_cols.T, mapped, precision=lax.Precision.HIGHEST), None)
    q_sum, unused = lax.scan(q_step, jnp.zeros((TAPS * CIN, RANK), jnp.float32), (latent_in, out_grad))
    q_factor = (q_sum / COUT).reshape(TAPS, CIN, RANK)
    return (p_factor, q_factor)
```

```python
import math

import jax
import jax.numpy as jnp
from jax import lax
from jax.experimental import pallas as pl
from jax.experimental.pallas import tpu as pltpu
from jax.sharding import Mesh
from jax.sharding import PartitionSpec as P

F32 = jnp.float32
BF16 = jnp.bfloat16
VMEM = pl.BlockSpec(memory_space=pltpu.VMEM)
ANY = pl.BlockSpec(memory_space=pl.ANY)


def parts_of(value):
    high = value.astype(BF16)
    rest = value - high.astype(F32)
    middle = rest.astype(BF16)
    low = (rest - middle.astype(F32)).astype(BF16)
    return high, middle, low


def dot(left, right, dims):
    return lax.dot_general(left, right, (dims, ((), ())), preferred_element_type=F32)


def left_kernel(width, x_ref, g_hbm, q_ref, out_ref, g_ref, sem):
    load = pltpu.make_async_copy(g_hbm, g_ref, sem)
    load.start()
    pixels, rank = g_ref.shape[0], q_ref.shape[2]
    taps = None
    for a in range(3):
        basis = jnp.concatenate([q_ref[3 * a + b] for b in range(3)], axis=1)
        term = dot(x_ref[width * a : width * a + pixels, :], basis, ((1,), (0,)))
        taps = term if taps is None else taps + term
    column = lax.broadcasted_iota(jnp.int32, (pixels, rank), 0) & (width - 1)
    before = pltpu.roll(taps[:, :rank], 1, 0)
    after = pltpu.roll(taps[:, 2 * rank :], pixels - 1, 0)
    projected = (
        taps[:, rank : 2 * rank]
        + jnp.where(column == 0, 0.0, before)
        + jnp.where(column == width - 1, 0.0, after)
    )
    stacked = jnp.concatenate(parts_of(projected.T), axis=0)
    load.wait()
    total = dot(stacked, g_ref[...], ((1,), (0,)))
    total = total[:rank] + total[rank : 2 * rank] + total[2 * rank :]
    rows = out_ref.shape[1]
    for i in range(out_ref.shape[0]):
        out_ref[i] = total[rows * i : rows * (i + 1)]


def gather_rows(pieces_ref, whole_ref):
    rows = pieces_ref.shape[1]
    for i in range(pieces_ref.shape[0]):
        whole_ref[rows * i : rows * (i + 1), :] = pieces_ref[i]


def right_kernel(width, p_ref, x_ref, g_hbm, out_ref, whole_ref, g_ref, sem):
    load = pltpu.make_async_copy(g_hbm, g_ref, sem)
    load.start()
    gather_rows(p_ref, whole_ref)
    rank, pixels = whole_ref.shape[0], g_ref.shape[0]
    cin = x_ref.shape[1]
    stacked = jnp.concatenate(parts_of(whole_ref[...]), axis=0)
    load.wait()
    mapped = dot(stacked, g_ref[...], ((1,), (1,)))
    mapped = mapped[:rank] + mapped[rank : 2 * rank] + mapped[2 * rank :]
    column = lax.broadcasted_iota(jnp.int32, (rank, pixels), 1) & (width - 1)
    ahead = jnp.where(column == width - 1, 0.0, pltpu.roll(mapped, pixels - 1, 1))
    behind = jnp.where(column == 0, 0.0, pltpu.roll(mapped, 1, 1))
    shifted = jnp.concatenate(
        [part for side in (ahead, mapped, behind) for part in parts_of(side)], axis=0
    )
    pieces = []
    for a in range(3):
        term = dot(shifted, x_ref[width * a : width * a + pixels, :], ((1,), (0,)))
        for b in range(3):
            t = term[3 * rank * b : 3 * rank * (b + 1)]
            pieces.append(t[:rank] + t[rank : 2 * rank] + t[2 * rank :])
    whole = jnp.concatenate(pieces, axis=1)
    groups, rows = out_ref.shape[0], out_ref.shape[1]
    for i in range(groups):
        out_ref[i] = whole[rows * i : rows * (i + 1)]


def factor_kernel(scale, p_ref, inverse_ref, factor_ref, whole_ref):
    gather_rows(p_ref, whole_ref)
    whole = whole_ref[...]
    rank = whole.shape[0]
    gram = lax.dot_general(
        whole,
        whole,
        (((1,), (1,)), ((), ())),
        precision=lax.Precision.HIGHEST,
        preferred_element_type=F32,
    )
    row = lax.broadcasted_iota(jnp.int32, (rank, rank), 0)
    col = lax.broadcasted_iota(jnp.int32, (rank, rank), 1)
    eye = row == col
    work = jnp.concatenate([gram, jnp.where(eye, 1.0, 0.0)], axis=1)
    below = lax.broadcasted_iota(jnp.int32, (rank, 1), 0)
    for j in range(rank - 1):
        pivot_row = work[j : j + 1, :]
        pivot_row = pivot_row / work[j : j + 1, j : j + 1]
        multiplier = jnp.where(below > j, work[:, j : j + 1], 0.0)
        work = work - multiplier * pivot_row
    diagonal = jnp.sum(jnp.where(eye, work[:, :rank], 0.0), axis=1, keepdims=True)
    inverse = work[:, rank:] / jnp.sqrt(diagonal)
    inverse_ref[...] = inverse
    rows = lax.dot_general(
        inverse,
        whole,
        (((1,), (0,)), ((), ())),
        precision=lax.Precision.HIGHEST,
        preferred_element_type=F32,
    )
    factor_ref[...] = (scale * rows).T


def finish_kernel(scale, q_ref, inverse_ref, out_ref):
    groups = q_ref.shape[0]
    raw = jnp.concatenate([q_ref[i] for i in range(groups)], axis=0)
    high, middle, low = parts_of(raw)
    inv_high, inv_middle, inv_low = parts_of(inverse_ref[...])
    left = jnp.concatenate([inv_high, inv_middle, inv_high, inv_high], axis=1)
    right = jnp.concatenate([high, high, middle, low], axis=0)
    out_ref[...] = (scale * dot(left, right, ((1,), (0,)))).T


def solution(mesh):
    n_x, n_z, n_y, n_c = 4, 16, 4, 2
    grid = Mesh(mesh.devices.reshape(n_x, n_z, n_y, n_c), ("x", "z", "y", "c"))
    planes = ("x", "y", "c")
    n_plane = n_x * n_y * n_c

    def call(kernel, out_shape, in_specs, scratch, flops, moved):
        return pl.pallas_call(
            kernel,
            out_shape=out_shape,
            in_specs=in_specs,
            out_specs=jax.tree.map(lambda _: VMEM, out_shape),
            scratch_shapes=scratch,
            compiler_params=pltpu.CompilerParams(vmem_limit_bytes=40 * 2**20),
            cost_estimate=pl.CostEstimate(flops=flops, bytes_accessed=moved, transcendentals=0),
        )

    def exchange(blocks, axes):
        return lax.all_to_all(blocks, axes, 0, 0, tiled=True)

    def to_all(block, axes, count):
        return exchange(jnp.broadcast_to(block[None], (count,) + block.shape), axes)

    def body(latent_in, out_grad, q_prev):
        rows, width, cout = out_grad.shape[1:]
        taps, cin, rank = q_prev.shape
        pixels = rows * width
        x = latent_in.reshape(-1, cin)
        g = out_grad.reshape(pixels, cout)
        g_scratch = [pltpu.VMEM((pixels, cout), BF16), pltpu.SemaphoreType.DMA]
        whole_p = pltpu.VMEM((rank, cout), F32)
        own = rank // n_plane

        p_term = call(
            lambda *refs: left_kernel(width, *refs),
            jax.ShapeDtypeStruct((n_plane, own, cout), F32),
            [VMEM, ANY, VMEM],
            g_scratch,
            2 * pixels * cout * 256,
            2 * pixels * cout,
        )(x, g, q_prev)
        piece = jnp.sum(exchange(p_term, planes), axis=0)
        piece = jnp.sum(to_all(piece, "z", n_z), axis=0)
        p_pieces = to_all(piece, planes, n_plane)

        q_term = call(
            lambda *refs: right_kernel(width, *refs),
            jax.ShapeDtypeStruct((n_x, rank // n_x, taps * cin), F32),
            [VMEM, VMEM, ANY],
            [whole_p] + g_scratch,
            4 * pixels * cout * 256,
            2 * pixels * cout,
        )(p_pieces, x, g)

        inverse, p_whole = call(
            lambda *refs: factor_kernel(math.sqrt(cout), *refs),
            (jax.ShapeDtypeStruct((rank, rank), F32), jax.ShapeDtypeStruct((cout, rank), F32)),
            [VMEM],
            [whole_p],
            2 * pixels * cout * 256,
            2 * pixels * cout,
        )(p_pieces)
        share = cout // (n_x * n_z)
        at = (lax.axis_index("x") * n_z + lax.axis_index("z")) * share
        p_factor = lax.dynamic_slice_in_dim(p_whole, at, share, axis=0)

        part = jnp.sum(exchange(q_term, "x"), axis=0)
        part = part.reshape(n_z, rank // (n_x * n_z), taps * cin)
        part = jnp.sum(exchange(part, "z"), axis=0)
        part = to_all(part, "z", n_z).reshape(rank // n_x, taps * cin)
        q_raw = to_all(part, "x", n_x)

        q_factor = call(
            lambda *refs: finish_kernel(1.0 / math.sqrt(cout), *refs),
            jax.ShapeDtypeStruct((taps * cin, rank), F32),
            [VMEM, VMEM],
            [],
            2 * taps * cin * rank * 256,
            8 * taps * cin * rank,
        )(q_raw, inverse)
        return p_factor, q_factor.reshape(taps, cin, rank)

    sample, channel = ("x", "z"), ("y", "c")
    return jax.shard_map(
        body,
        mesh=grid,
        in_specs=(P(sample, None, None, channel), P(sample, None, None, None), P(None, channel, None)),
        out_specs=(P(sample, None), P(None, channel, None)),
        check_vma=False,
    )
```

```python
import math

import jax
import jax.numpy as jnp
from jax import lax
from jax.experimental import pallas as pl
from jax.experimental.pallas import tpu as pltpu
from jax.sharding import Mesh
from jax.sharding import PartitionSpec as P

F32 = jnp.float32
BF16 = jnp.bfloat16
VMEM = pl.BlockSpec(memory_space=pltpu.VMEM)
HBM = pl.BlockSpec(memory_space=pltpu.HBM)


def parts_of(value):
    high = value.astype(BF16)
    rest = value - high.astype(F32)
    middle = rest.astype(BF16)
    low = (rest - middle.astype(F32)).astype(BF16)
    return high, middle, low


def dot(left, right, dims):
    return lax.dot_general(left, right, (dims, ((), ())), preferred_element_type=F32)


def left_kernel(width, x_hbm, q_hbm, g_hbm, out_ref, x_ref, q_ref, g_ref, sems):
    loads = [
        pltpu.make_async_copy(source, target, sems.at[i])
        for i, (source, target) in enumerate(((x_hbm, x_ref), (q_hbm, q_ref), (g_hbm, g_ref)))
    ]
    for load in loads:
        load.start()
    loads[0].wait()
    loads[1].wait()
    pixels, rank, cin = g_ref.shape[0], q_ref.shape[1], q_ref.shape[2]
    taps = None
    for a in range(3):
        basis = q_ref[3 * a : 3 * a + 3].reshape(3 * rank, cin)
        term = dot(basis, x_ref[width * a : width * a + pixels, :], ((1,), (1,)))
        taps = term if taps is None else taps + term
    column = lax.broadcasted_iota(jnp.int32, (rank, pixels), 1) & (width - 1)
    before = pltpu.roll(taps[:rank], 1, 1)
    after = pltpu.roll(taps[2 * rank :], pixels - 1, 1)
    projected = (
        taps[rank : 2 * rank]
        + jnp.where(column == 0, 0.0, before)
        + jnp.where(column == width - 1, 0.0, after)
    )
    stacked = jnp.concatenate(parts_of(projected), axis=0)
    loads[2].wait()
    total = dot(stacked, g_ref[...], ((1,), (0,)))
    total = total[:rank] + total[rank : 2 * rank] + total[2 * rank :]
    rows = out_ref.shape[1]
    for i in range(out_ref.shape[0]):
        out_ref[i] = total[rows * i : rows * (i + 1)]


def gather_rows(pieces_ref, whole_ref):
    rows = pieces_ref.shape[1]
    for i in range(pieces_ref.shape[0]):
        whole_ref[rows * i : rows * (i + 1), :] = pieces_ref[i]


def right_kernel(width, p_ref, x_ref, g_ref, out_ref, whole_ref):
    gather_rows(p_ref, whole_ref)
    rank, pixels = whole_ref.shape[0], g_ref.shape[0]
    stacked = jnp.concatenate(parts_of(whole_ref[...]), axis=0)
    mapped = dot(stacked, g_ref[...], ((1,), (1,)))
    mapped = mapped[:rank] + mapped[rank : 2 * rank] + mapped[2 * rank :]
    column = lax.broadcasted_iota(jnp.int32, (rank, pixels), 1) & (width - 1)
    ahead = jnp.where(column == width - 1, 0.0, pltpu.roll(mapped, pixels - 1, 1))
    behind = jnp.where(column == 0, 0.0, pltpu.roll(mapped, 1, 1))
    shifted = jnp.concatenate(
        [part for side in (ahead, mapped, behind) for part in parts_of(side)], axis=0
    )
    pieces = []
    for a in range(3):
        term = dot(shifted, x_ref[width * a : width * a + pixels, :], ((1,), (0,)))
        for b in range(3):
            t = term[3 * rank * b : 3 * rank * (b + 1)]
            pieces.append(t[:rank] + t[rank : 2 * rank] + t[2 * rank :])
    whole = jnp.concatenate(pieces, axis=1)
    groups, rows = out_ref.shape[0], out_ref.shape[1]
    for i in range(groups):
        out_ref[i] = whole[rows * i : rows * (i + 1)]


def factor_kernel(scale, p_ref, inverse_ref, factor_ref, whole_ref):
    gather_rows(p_ref, whole_ref)
    whole = whole_ref[...]
    rank = whole.shape[0]
    gram = lax.dot_general(
        whole,
        whole,
        (((1,), (1,)), ((), ())),
        precision=lax.Precision.HIGHEST,
        preferred_element_type=F32,
    )
    row = lax.broadcasted_iota(jnp.int32, (rank, rank), 0)
    col = lax.broadcasted_iota(jnp.int32, (rank, rank), 1)
    eye = row == col
    work = jnp.concatenate([gram, jnp.where(eye, 1.0, 0.0)], axis=1)
    below = lax.broadcasted_iota(jnp.int32, (rank, 1), 0)
    for j in range(rank - 1):
        pivot_row = work[j : j + 1, :]
        pivot_row = pivot_row / work[j : j + 1, j : j + 1]
        multiplier = jnp.where(below > j, work[:, j : j + 1], 0.0)
        work = work - multiplier * pivot_row
    diagonal = jnp.sum(jnp.where(eye, work[:, :rank], 0.0), axis=1, keepdims=True)
    inverse = work[:, rank:] / jnp.sqrt(diagonal)
    inverse_ref[...] = inverse
    rows = lax.dot_general(
        inverse,
        whole,
        (((1,), (0,)), ((), ())),
        precision=lax.Precision.HIGHEST,
        preferred_element_type=F32,
    )
    factor_ref[...] = (scale * rows).T


def finish_kernel(scale, q_ref, inverse_ref, out_ref):
    groups = q_ref.shape[0]
    raw = jnp.concatenate([q_ref[i] for i in range(groups)], axis=0)
    high, middle, low = parts_of(raw)
    inv_high, inv_middle, inv_low = parts_of(inverse_ref[...])
    left = jnp.concatenate([inv_high, inv_middle, inv_high, inv_high], axis=1)
    right = jnp.concatenate([high, high, middle, low], axis=0)
    whole = scale * dot(left, right, ((1,), (0,)))
    cin = out_ref.shape[2]
    for k in range(out_ref.shape[0]):
        out_ref[k] = whole[:, cin * k : cin * (k + 1)]


def solution(mesh):
    sizes = {"x": 4, "far": 8, "near": 2, "y": 4, "c": 2}
    grid = Mesh(mesh.devices.reshape(tuple(sizes.values())), tuple(sizes))

    def count(axes):
        return math.prod(sizes[axis] for axis in axes)

    sample, channel = ("x", "far", "near"), ("y", "c")
    p_split, q_split, rest = ("x", "near", "y", "c"), ("x", "near"), ("far",)

    def call(kernel, out_shape, in_specs, scratch, flops, moved, grant=40):
        return pl.pallas_call(
            kernel,
            out_shape=out_shape,
            in_specs=in_specs,
            out_specs=jax.tree.map(lambda _: VMEM, out_shape),
            scratch_shapes=scratch,
            compiler_params=pltpu.CompilerParams(vmem_limit_bytes=grant * 2**20),
            cost_estimate=pl.CostEstimate(flops=flops, bytes_accessed=moved, transcendentals=0),
        )

    def exchange(blocks, axes):
        return lax.all_to_all(blocks, axes, 0, 0, tiled=True)

    def to_all(block, axes):
        return exchange(jnp.broadcast_to(block[None], (count(axes),) + block.shape), axes)

    def body(latent_in, out_grad, q_prev):
        rows, width, cout = out_grad.shape[1:]
        taps, cin, rank = q_prev.shape
        pixels = rows * width
        x = latent_in.reshape(-1, cin)
        g = out_grad.reshape(pixels, cout)
        q_turned = jnp.swapaxes(q_prev, 1, 2)
        loaded = [pltpu.VMEM(array.shape, BF16) for array in (x, q_turned, g)]
        whole_p = pltpu.VMEM((rank, cout), F32)

        p_term = call(
            lambda *refs: left_kernel(width, *refs),
            jax.ShapeDtypeStruct((count(p_split), rank // count(p_split), cout), F32),
            [HBM, HBM, HBM],
            loaded + [pltpu.SemaphoreType.DMA((3,))],
            2 * pixels * cout * 256,
            2 * pixels * cout,
            grant=60,
        )(x, q_turned, g)
        piece = jnp.sum(exchange(p_term, p_split), axis=0)
        piece, x_again, g_again = lax.optimization_barrier((piece, x, g))
        piece = jnp.sum(to_all(piece, rest), axis=0)
        p_pieces = to_all(piece, p_split)

        q_term = call(
            lambda *refs: right_kernel(width, *refs),
            jax.ShapeDtypeStruct((count(q_split), rank // count(q_split), taps * cin), F32),
            [VMEM, VMEM, VMEM],
            [whole_p],
            4 * pixels * cout * 256,
            2 * pixels * cout,
        )(p_pieces, x_again, g_again)

        part = jnp.sum(exchange(q_term, q_split), axis=0)
        part, p_again = lax.optimization_barrier((part, p_pieces))
        inverse, p_whole = call(
            lambda *refs: factor_kernel(math.sqrt(cout), *refs),
            (jax.ShapeDtypeStruct((rank, rank), F32), jax.ShapeDtypeStruct((cout, rank), F32)),
            [VMEM],
            [whole_p],
            2 * pixels * cout * 256,
            2 * pixels * cout,
        )(p_again)
        share = cout // count(sample)
        at = lax.axis_index(sample) * share
        p_factor = lax.dynamic_slice_in_dim(p_whole, at, share, axis=0)
        part = jnp.sum(to_all(part, rest), axis=0)
        part, inverse, p_factor = lax.optimization_barrier((part, inverse, p_factor))
        q_raw = to_all(part, q_split)

        q_factor = call(
            lambda *refs: finish_kernel(1.0 / math.sqrt(cout), *refs),
            jax.ShapeDtypeStruct((taps, rank, cin), F32),
            [VMEM, VMEM],
            [],
            2 * taps * cin * rank * 256,
            8 * taps * cin * rank,
        )(q_raw, inverse)
        return p_factor, jnp.swapaxes(q_factor, 1, 2)

    return jax.shard_map(
        body,
        mesh=grid,
        in_specs=(P(sample, None, None, channel), P(sample, None, None, None), P(None, channel, None)),
        out_specs=(P(sample, None), P(None, channel, None)),
        check_vma=False,
    )
```

```python
import itertools
import math

import jax
import jax.numpy as jnp
from jax import lax
from jax.experimental import pallas as pl
from jax.experimental.pallas import tpu as pltpu
from jax.sharding import Mesh
from jax.sharding import PartitionSpec as P

F32 = jnp.float32
BF16 = jnp.bfloat16
VMEM = pl.BlockSpec(memory_space=pltpu.VMEM)
HBM = pl.BlockSpec(memory_space=pltpu.HBM)


def parts_of(value):
    high = value.astype(BF16)
    rest = value - high.astype(F32)
    middle = rest.astype(BF16)
    low = (rest - middle.astype(F32)).astype(BF16)
    return high, middle, low


def dot(left, right, dims):
    return lax.dot_general(left, right, (dims, ((), ())), preferred_element_type=F32)


def left_kernel(width, x_hbm, q_hbm, g_hbm, out_ref, x_ref, g_ref, q_ref, sems):
    loads = [
        pltpu.make_async_copy(source, target, sems.at[i])
        for i, (source, target) in enumerate(((x_hbm, x_ref), (q_hbm, q_ref), (g_hbm, g_ref)))
    ]
    for load in loads:
        load.start()
    loads[0].wait()
    loads[1].wait()
    pixels, rank, cin = g_ref.shape[0], q_ref.shape[1], q_ref.shape[2]
    taps = None
    for a in range(3):
        basis = q_ref[3 * a : 3 * a + 3].reshape(3 * rank, cin)
        term = dot(basis, x_ref[width * a : width * a + pixels, :], ((1,), (1,)))
        taps = term if taps is None else taps + term
    column = lax.broadcasted_iota(jnp.int32, (rank, pixels), 1) & (width - 1)
    before = pltpu.roll(taps[:rank], 1, 1)
    after = pltpu.roll(taps[2 * rank :], pixels - 1, 1)
    projected = (
        taps[rank : 2 * rank]
        + jnp.where(column == 0, 0.0, before)
        + jnp.where(column == width - 1, 0.0, after)
    )
    stacked = jnp.concatenate(parts_of(projected), axis=0)
    loads[2].wait()
    total = dot(stacked, g_ref[...], ((1,), (0,)))
    total = total[:rank] + total[rank : 2 * rank] + total[2 * rank :]
    rows = out_ref.shape[1]
    for i in range(out_ref.shape[0]):
        out_ref[i] = total[rows * i : rows * (i + 1)]


def gather_rows(pieces_ref, whole_ref):
    rows = pieces_ref.shape[1]
    for i in range(pieces_ref.shape[0]):
        whole_ref[rows * i : rows * (i + 1), :] = pieces_ref[i]


def right_kernel(width, p_ref, x_ref, g_ref, out_ref, whole_ref):
    gather_rows(p_ref, whole_ref)
    rank, pixels = whole_ref.shape[0], g_ref.shape[0]
    stacked = jnp.concatenate(parts_of(whole_ref[...]), axis=0)
    mapped = dot(stacked, g_ref[...], ((1,), (1,)))
    mapped = mapped[:rank] + mapped[rank : 2 * rank] + mapped[2 * rank :]
    column = lax.broadcasted_iota(jnp.int32, (rank, pixels), 1) & (width - 1)
    ahead = jnp.where(column == width - 1, 0.0, pltpu.roll(mapped, pixels - 1, 1))
    behind = jnp.where(column == 0, 0.0, pltpu.roll(mapped, 1, 1))
    shifted = jnp.concatenate(
        [part for side in (ahead, mapped, behind) for part in parts_of(side)], axis=0
    )
    pieces = []
    for a in range(3):
        term = dot(shifted, x_ref[width * a : width * a + pixels, :], ((1,), (0,)))
        for b in range(3):
            t = term[3 * rank * b : 3 * rank * (b + 1)]
            pieces.append(t[:rank] + t[rank : 2 * rank] + t[2 * rank :])
    whole = jnp.concatenate(pieces, axis=1)
    groups, rows = out_ref.shape[0], out_ref.shape[1]
    for i in range(groups):
        out_ref[i] = whole[rows * i : rows * (i + 1)]


def factor_kernel(scale, p_ref, inverse_ref, factor_ref, whole_ref):
    gather_rows(p_ref, whole_ref)
    whole = whole_ref[...]
    rank = whole.shape[0]
    gram = lax.dot_general(
        whole,
        whole,
        (((1,), (1,)), ((), ())),
        precision=lax.Precision.HIGHEST,
        preferred_element_type=F32,
    )
    row = lax.broadcasted_iota(jnp.int32, (rank, rank), 0)
    col = lax.broadcasted_iota(jnp.int32, (rank, rank), 1)
    eye = row == col
    work = jnp.concatenate([gram, jnp.where(eye, 1.0, 0.0)], axis=1)
    below = lax.broadcasted_iota(jnp.int32, (rank, 1), 0)
    for j in range(rank - 1):
        pivot_row = work[j : j + 1, :]
        pivot_row = pivot_row / work[j : j + 1, j : j + 1]
        multiplier = jnp.where(below > j, work[:, j : j + 1], 0.0)
        work = work - multiplier * pivot_row
    diagonal = jnp.sum(jnp.where(eye, work[:, :rank], 0.0), axis=1, keepdims=True)
    inverse = work[:, rank:] / jnp.sqrt(diagonal)
    inverse_ref[...] = inverse
    rows = lax.dot_general(
        inverse,
        whole,
        (((1,), (0,)), ((), ())),
        precision=lax.Precision.HIGHEST,
        preferred_element_type=F32,
    )
    factor_ref[...] = (scale * rows).T


def finish_kernel(scale, q_ref, inverse_ref, out_ref):
    groups = q_ref.shape[0]
    raw = jnp.concatenate([q_ref[i] for i in range(groups)], axis=0)
    high, middle, low = parts_of(raw)
    inv_high, inv_middle, inv_low = parts_of(inverse_ref[...])
    left = jnp.concatenate([inv_high, inv_middle, inv_high, inv_high], axis=1)
    right = jnp.concatenate([high, high, middle, low], axis=0)
    whole = scale * dot(left, right, ((1,), (0,)))
    cin = out_ref.shape[2]
    for k in range(out_ref.shape[0]):
        out_ref[k] = whole[:, cin * k : cin * (k + 1)]


def solution(mesh):
    sizes = {"x": 4, "far": 4, "middle": 2, "near": 2, "y": 4, "c": 2}
    grid = Mesh(mesh.devices.reshape(tuple(sizes.values())), tuple(sizes))

    def count(axes):
        return math.prod(sizes[axis] for axis in axes)

    sample, channel = ("x", "far", "middle", "near"), ("y", "c")
    p_split, p_rest = ("x", "near", "y", "c"), ("far", "middle")
    q_split, q_rest = ("x", "middle", "near"), ("far",)

    first = {"far": 2, "x": 2, "y": 2, "near": 1}

    def call(kernel, out_shape, in_specs, scratch, flops, moved, grant=40):
        return pl.pallas_call(
            kernel,
            out_shape=out_shape,
            in_specs=in_specs,
            out_specs=jax.tree.map(lambda _: VMEM, out_shape),
            scratch_shapes=scratch,
            compiler_params=pltpu.CompilerParams(vmem_limit_bytes=grant * 2**20),
            cost_estimate=pl.CostEstimate(flops=flops, bytes_accessed=moved, transcendentals=0),
        )

    def groups_of(axes):
        others = [axis for axis in sizes if axis not in axes]
        groups = []
        for place in itertools.product(*(range(sizes[axis]) for axis in others)):
            group = []
            for steps in itertools.product(*(range(sizes[axis]) for axis in axes)):
                at = dict(zip(others, place))
                for axis, step in zip(axes, steps):
                    at[axis] = (step + first.get(axis, 0)) % sizes[axis]
                index = 0
                for axis, size in sizes.items():
                    index = index * size + at[axis]
                group.append(index)
            groups.append(group)
        return groups

    def exchange(blocks, axes):
        if any(axis in first for axis in axes):
            return lax.all_to_all(
                blocks, tuple(sizes), 0, 0, tiled=True, axis_index_groups=groups_of(axes)
            )
        return lax.all_to_all(blocks, axes, 0, 0, tiled=True)

    def to_all(block, axes):
        return exchange(jnp.broadcast_to(block[None], (count(axes),) + block.shape), axes)

    def body(latent_in, out_grad, q_prev):
        rows, width, cout = out_grad.shape[1:]
        taps, cin, rank = q_prev.shape
        pixels = rows * width
        x = latent_in.reshape(-1, cin)
        g = out_grad.reshape(pixels, cout)
        q_turned = jnp.swapaxes(q_prev, 1, 2)
        whole_p = pltpu.VMEM((rank, cout), F32)

        p_term, x_held, g_held = call(
            lambda *refs: left_kernel(width, *refs),
            (
                jax.ShapeDtypeStruct((count(p_split), rank // count(p_split), cout), F32),
                jax.ShapeDtypeStruct(x.shape, BF16),
                jax.ShapeDtypeStruct(g.shape, BF16),
            ),
            [HBM, HBM, HBM],
            [pltpu.VMEM(q_turned.shape, BF16), pltpu.SemaphoreType.DMA((3,))],
            2 * pixels * cout * 256,
            2 * pixels * cout,
            grant=16,
        )(*(pltpu.with_memory_space_constraint(array, pltpu.HBM) for array in (x, q_turned, g)))
        piece = jnp.sum(exchange(p_term, p_split), axis=0)
        piece = jnp.sum(to_all(piece, p_rest), axis=0)
        p_pieces = to_all(piece, p_split)

        q_term = call(
            lambda *refs: right_kernel(width, *refs),
            jax.ShapeDtypeStruct((count(q_split), rank // count(q_split), taps * cin), F32),
            [VMEM, VMEM, VMEM],
            [whole_p],
            4 * pixels * cout * 256,
            2 * pixels * cout,
        )(p_pieces, x_held, g_held)

        part = jnp.sum(exchange(q_term, q_split), axis=0)
        inverse, p_whole = call(
            lambda *refs: factor_kernel(math.sqrt(cout), *refs),
            (jax.ShapeDtypeStruct((rank, rank), F32), jax.ShapeDtypeStruct((cout, rank), F32)),
            [VMEM],
            [whole_p],
            2 * pixels * cout * 256,
            2 * pixels * cout,
        )(p_pieces)
        share = cout // count(sample)
        at = lax.axis_index(sample) * share
        p_factor = lax.dynamic_slice_in_dim(p_whole, at, share, axis=0)
        part, inverse, p_factor = lax.optimization_barrier((part, inverse, p_factor))
        part = jnp.sum(to_all(part, q_rest), axis=0)
        q_raw = to_all(part, q_split)

        q_factor = call(
            lambda *refs: finish_kernel(1.0 / math.sqrt(cout), *refs),
            jax.ShapeDtypeStruct((taps, rank, cin), F32),
            [VMEM, VMEM],
            [],
            2 * taps * cin * rank * 256,
            8 * taps * cin * rank,
        )(q_raw, inverse)
        return p_factor, jnp.swapaxes(q_factor, 1, 2)

    return jax.shard_map(
        body,
        mesh=grid,
        in_specs=(P(sample, None, None, channel), P(sample, None, None, None), P(None, channel, None)),
        out_specs=(P(sample, None), P(None, channel, None)),
        check_vma=False,
    )
```

```python
import itertools
import math

import jax
import jax.numpy as jnp
from jax import lax
from jax.experimental import pallas as pl
from jax.experimental.pallas import tpu as pltpu
from jax.sharding import Mesh
from jax.sharding import PartitionSpec as P

F32 = jnp.float32
BF16 = jnp.bfloat16
VMEM = pl.BlockSpec(memory_space=pltpu.VMEM)
HBM = pl.BlockSpec(memory_space=pltpu.HBM)


def parts_of(value):
    high = value.astype(BF16)
    rest = value - high.astype(F32)
    middle = rest.astype(BF16)
    low = (rest - middle.astype(F32)).astype(BF16)
    return high, middle, low


def dot(left, right, dims):
    return lax.dot_general(left, right, (dims, ((), ())), preferred_element_type=F32)


def left_kernel(width, x_hbm, q_hbm, g_hbm, out_ref, x_ref, g_ref, q_ref, sems):
    loads = [
        pltpu.make_async_copy(source, target, sems.at[i])
        for i, (source, target) in enumerate(((x_hbm, x_ref), (q_hbm, q_ref), (g_hbm, g_ref)))
    ]
    for load in loads:
        load.start()
    loads[0].wait()
    loads[1].wait()
    pixels, rank, cin = g_ref.shape[0], q_ref.shape[1], q_ref.shape[2]
    taps = None
    for a in range(3):
        basis = q_ref[3 * a : 3 * a + 3].reshape(3 * rank, cin)
        term = dot(basis, x_ref[width * a : width * a + pixels, :], ((1,), (1,)))
        taps = term if taps is None else taps + term
    column = lax.broadcasted_iota(jnp.int32, (rank, pixels), 1) & (width - 1)
    before = pltpu.roll(taps[:rank], 1, 1)
    after = pltpu.roll(taps[2 * rank :], pixels - 1, 1)
    projected = (
        taps[rank : 2 * rank]
        + jnp.where(column == 0, 0.0, before)
        + jnp.where(column == width - 1, 0.0, after)
    )
    stacked = jnp.concatenate(parts_of(projected), axis=0)
    loads[2].wait()
    total = dot(stacked, g_ref[...], ((1,), (0,)))
    total = total[:rank] + total[rank : 2 * rank] + total[2 * rank :]
    rows = out_ref.shape[1]
    for i in range(out_ref.shape[0]):
        out_ref[i] = total[rows * i : rows * (i + 1)]


def gather_rows(pieces_ref, whole_ref):
    rows = pieces_ref.shape[1]
    for i in range(pieces_ref.shape[0]):
        whole_ref[rows * i : rows * (i + 1), :] = pieces_ref[i]


def right_kernel(width, p_ref, x_ref, g_ref, out_ref, whole_ref):
    gather_rows(p_ref, whole_ref)
    rank, pixels = whole_ref.shape[0], g_ref.shape[0]
    stacked = jnp.concatenate(parts_of(whole_ref[...]), axis=0)
    mapped = dot(stacked, g_ref[...], ((1,), (1,)))
    mapped = mapped[:rank] + mapped[rank : 2 * rank] + mapped[2 * rank :]
    column = lax.broadcasted_iota(jnp.int32, (rank, pixels), 1) & (width - 1)
    ahead = jnp.where(column == width - 1, 0.0, pltpu.roll(mapped, pixels - 1, 1))
    behind = jnp.where(column == 0, 0.0, pltpu.roll(mapped, 1, 1))
    shifted = jnp.concatenate(
        [part for side in (ahead, mapped, behind) for part in parts_of(side)], axis=0
    )
    pieces = []
    for a in range(3):
        term = dot(shifted, x_ref[width * a : width * a + pixels, :], ((1,), (0,)))
        for b in range(3):
            t = term[3 * rank * b : 3 * rank * (b + 1)]
            pieces.append(t[:rank] + t[rank : 2 * rank] + t[2 * rank :])
    whole = jnp.concatenate(pieces, axis=1)
    groups, rows = out_ref.shape[0], out_ref.shape[1]
    for i in range(groups):
        out_ref[i] = whole[rows * i : rows * (i + 1)]


def factor_kernel(scale, p_ref, inverse_ref, factor_ref, whole_ref):
    gather_rows(p_ref, whole_ref)
    whole = whole_ref[...]
    rank = whole.shape[0]
    gram = lax.dot_general(
        whole,
        whole,
        (((1,), (1,)), ((), ())),
        precision=lax.Precision.HIGHEST,
        preferred_element_type=F32,
    )
    row = lax.broadcasted_iota(jnp.int32, (rank, rank), 0)
    col = lax.broadcasted_iota(jnp.int32, (rank, rank), 1)
    eye = row == col
    work = jnp.concatenate([gram, jnp.where(eye, 1.0, 0.0)], axis=1)
    below = lax.broadcasted_iota(jnp.int32, (rank, 1), 0)
    for j in range(rank - 1):
        pivot_row = work[j : j + 1, :]
        pivot_row = pivot_row / work[j : j + 1, j : j + 1]
        multiplier = jnp.where(below > j, work[:, j : j + 1], 0.0)
        work = work - multiplier * pivot_row
    diagonal = jnp.sum(jnp.where(eye, work[:, :rank], 0.0), axis=1, keepdims=True)
    inverse = work[:, rank:] / jnp.sqrt(diagonal)
    inverse_ref[...] = inverse
    rows = lax.dot_general(
        inverse,
        whole,
        (((1,), (0,)), ((), ())),
        precision=lax.Precision.HIGHEST,
        preferred_element_type=F32,
    )
    factor_ref[...] = (scale * rows).T


def finish_kernel(scale, q_ref, inverse_ref, out_ref):
    groups = q_ref.shape[0]
    raw = jnp.concatenate([q_ref[i] for i in range(groups)], axis=0)
    high, middle, low = parts_of(raw)
    inv_high, inv_middle, inv_low = parts_of(inverse_ref[...])
    left = jnp.concatenate([inv_high, inv_middle, inv_high, inv_high], axis=1)
    right = jnp.concatenate([high, high, middle, low], axis=0)
    whole = scale * dot(left, right, ((1,), (0,)))
    cin = out_ref.shape[2]
    for k in range(out_ref.shape[0]):
        out_ref[k] = whole[:, cin * k : cin * (k + 1)]


def solution(mesh):
    sizes = {"x": 4, "far": 4, "middle": 2, "near": 2, "y": 4, "c": 2}
    grid = Mesh(mesh.devices.reshape(tuple(sizes.values())), tuple(sizes))

    def count(axes):
        return math.prod(sizes[axis] for axis in axes)

    sample, channel = ("x", "far", "middle", "near"), ("y", "c")
    p_split, p_rest = ("x", "near", "y", "c"), ("far", "middle")
    q_split, q_rest = ("x", "middle", "near"), ("far",)

    p_first, far_first = {"x": 2, "y": 2, "near": 1}, {"far": 2, "middle": 1}
    q_first, last_first = {"x": 2, "middle": 1}, {"far": 2}

    def call(kernel, out_shape, in_specs, scratch, flops, moved, grant=40):
        return pl.pallas_call(
            kernel,
            out_shape=out_shape,
            in_specs=in_specs,
            out_specs=jax.tree.map(lambda _: VMEM, out_shape),
            scratch_shapes=scratch,
            compiler_params=pltpu.CompilerParams(vmem_limit_bytes=grant * 2**20),
            cost_estimate=pl.CostEstimate(flops=flops, bytes_accessed=moved, transcendentals=0),
        )

    def groups_of(axes, first):
        others = [axis for axis in sizes if axis not in axes]
        groups = []
        for place in itertools.product(*(range(sizes[axis]) for axis in others)):
            group = []
            for steps in itertools.product(*(range(sizes[axis]) for axis in axes)):
                at = dict(zip(others, place))
                for axis, step in zip(axes, steps):
                    at[axis] = (step + first.get(axis, 0)) % sizes[axis]
                index = 0
                for axis, size in sizes.items():
                    index = index * size + at[axis]
                group.append(index)
            groups.append(group)
        return groups

    def exchange(blocks, axes, first):
        if any(axis in first for axis in axes):
            return lax.all_to_all(
                blocks, tuple(sizes), 0, 0, tiled=True, axis_index_groups=groups_of(axes, first)
            )
        return lax.all_to_all(blocks, axes, 0, 0, tiled=True)

    def to_all(block, axes, first):
        return exchange(jnp.broadcast_to(block[None], (count(axes),) + block.shape), axes, first)

    def body(latent_in, out_grad, q_prev):
        rows, width, cout = out_grad.shape[1:]
        taps, cin, rank = q_prev.shape
        pixels = rows * width
        x = latent_in.reshape(-1, cin)
        g = out_grad.reshape(pixels, cout)
        q_turned = jnp.swapaxes(q_prev, 1, 2)
        whole_p = pltpu.VMEM((rank, cout), F32)

        p_term, x_held, g_held = call(
            lambda *refs: left_kernel(width, *refs),
            (
                jax.ShapeDtypeStruct((count(p_split), rank // count(p_split), cout), F32),
                jax.ShapeDtypeStruct(x.shape, BF16),
                jax.ShapeDtypeStruct(g.shape, BF16),
            ),
            [HBM, HBM, HBM],
            [pltpu.VMEM(q_turned.shape, BF16), pltpu.SemaphoreType.DMA((3,))],
            2 * pixels * cout * 256,
            2 * pixels * cout,
            grant=16,
        )(*(pltpu.with_memory_space_constraint(array, pltpu.HBM) for array in (x, q_turned, g)))
        piece = jnp.sum(exchange(p_term, p_split, p_first), axis=0)
        piece = jnp.sum(to_all(piece, p_rest, far_first), axis=0)
        p_pieces = to_all(piece, p_split, p_first)

        q_term = call(
            lambda *refs: right_kernel(width, *refs),
            jax.ShapeDtypeStruct((count(q_split), rank // count(q_split), taps * cin), F32),
            [VMEM, VMEM, VMEM],
            [whole_p],
            4 * pixels * cout * 256,
            2 * pixels * cout,
        )(p_pieces, x_held, g_held)

        part = jnp.sum(exchange(q_term, q_split, q_first), axis=0)
        inverse, p_whole = call(
            lambda *refs: factor_kernel(math.sqrt(cout), *refs),
            (jax.ShapeDtypeStruct((rank, rank), F32), jax.ShapeDtypeStruct((cout, rank), F32)),
            [VMEM],
            [whole_p],
            2 * pixels * cout * 256,
            2 * pixels * cout,
        )(p_pieces)
        share = cout // count(sample)
        at = lax.axis_index(sample) * share
        p_factor = lax.dynamic_slice_in_dim(p_whole, at, share, axis=0)
        part, inverse, p_factor = lax.optimization_barrier((part, inverse, p_factor))
        part = jnp.sum(to_all(part, q_rest, last_first), axis=0)
        q_raw = to_all(part, q_split, q_first)

        q_factor = call(
            lambda *refs: finish_kernel(1.0 / math.sqrt(cout), *refs),
            jax.ShapeDtypeStruct((taps, rank, cin), F32),
            [VMEM, VMEM],
            [],
            2 * taps * cin * rank * 256,
            8 * taps * cin * rank,
        )(q_raw, inverse)
        return p_factor, jnp.swapaxes(q_factor, 1, 2)

    return jax.shard_map(
        body,
        mesh=grid,
        in_specs=(P(sample, None, None, channel), P(sample, None, None, None), P(None, channel, None)),
        out_specs=(P(sample, None), P(None, channel, None)),
        check_vma=False,
    )
```

```python
import itertools
import math

import jax
import jax.numpy as jnp
from jax import lax
from jax.experimental import pallas as pl
from jax.experimental.pallas import tpu as pltpu
from jax.sharding import Mesh
from jax.sharding import PartitionSpec as P

F32 = jnp.float32
BF16 = jnp.bfloat16
VMEM = pl.BlockSpec(memory_space=pltpu.VMEM)
HBM = pl.BlockSpec(memory_space=pltpu.HBM)


def parts_of(value):
    high = value.astype(BF16)
    rest = value - high.astype(F32)
    middle = rest.astype(BF16)
    low = (rest - middle.astype(F32)).astype(BF16)
    return high, middle, low


def dot(left, right, dims):
    return lax.dot_general(left, right, (dims, ((), ())), preferred_element_type=F32)


def left_kernel(width, x_hbm, q_hbm, g_hbm, out_ref, x_ref, g_ref, q_ref, sems):
    loads = [
        pltpu.make_async_copy(source, target, sems.at[i])
        for i, (source, target) in enumerate(((x_hbm, x_ref), (q_hbm, q_ref), (g_hbm, g_ref)))
    ]
    for load in loads:
        load.start()
    loads[0].wait()
    loads[1].wait()
    pixels, rank, cin = g_ref.shape[0], q_ref.shape[1], q_ref.shape[2]
    taps = None
    for a in range(3):
        basis = q_ref[3 * a : 3 * a + 3].reshape(3 * rank, cin)
        term = dot(basis, x_ref[width * a : width * a + pixels, :], ((1,), (1,)))
        taps = term if taps is None else taps + term
    column = lax.broadcasted_iota(jnp.int32, (rank, pixels), 1) & (width - 1)
    before = pltpu.roll(taps[:rank], 1, 1)
    after = pltpu.roll(taps[2 * rank :], pixels - 1, 1)
    projected = (
        taps[rank : 2 * rank]
        + jnp.where(column == 0, 0.0, before)
        + jnp.where(column == width - 1, 0.0, after)
    )
    stacked = jnp.concatenate(parts_of(projected)[:2], axis=0)
    loads[2].wait()
    total = dot(stacked, g_ref[...], ((1,), (0,)))
    total = total[:rank] + total[rank:]
    rows = out_ref.shape[1]
    for i in range(out_ref.shape[0]):
        out_ref[i] = total[rows * i : rows * (i + 1)]


def gather_rows(pieces_ref, whole_ref):
    rows = pieces_ref.shape[1]
    for i in range(pieces_ref.shape[0]):
        whole_ref[rows * i : rows * (i + 1), :] = pieces_ref[i]


def right_kernel(width, p_ref, x_ref, g_ref, out_ref, whole_ref):
    gather_rows(p_ref, whole_ref)
    rank, pixels = whole_ref.shape[0], g_ref.shape[0]
    stacked = jnp.concatenate(parts_of(whole_ref[...])[:2], axis=0)
    mapped = dot(stacked, g_ref[...], ((1,), (1,)))
    mapped = mapped[:rank] + mapped[rank:]
    column = lax.broadcasted_iota(jnp.int32, (rank, pixels), 1) & (width - 1)
    ahead = jnp.where(column == width - 1, 0.0, pltpu.roll(mapped, pixels - 1, 1))
    behind = jnp.where(column == 0, 0.0, pltpu.roll(mapped, 1, 1))
    shifted = jnp.concatenate(
        [part for side in (ahead, mapped, behind) for part in parts_of(side)[:2]], axis=0
    )
    pieces = []
    for a in range(3):
        term = dot(shifted, x_ref[width * a : width * a + pixels, :], ((1,), (0,)))
        for b in range(3):
            t = term[2 * rank * b : 2 * rank * (b + 1)]
            pieces.append(t[:rank] + t[rank:])
    whole = jnp.concatenate(pieces, axis=1)
    groups, rows = out_ref.shape[0], out_ref.shape[1]
    for i in range(groups):
        out_ref[i] = whole[rows * i : rows * (i + 1)]


def factor_kernel(scale, p_ref, inverse_ref, factor_ref, whole_ref):
    gather_rows(p_ref, whole_ref)
    whole = whole_ref[...]
    rank = whole.shape[0]
    gram = lax.dot_general(
        whole,
        whole,
        (((1,), (1,)), ((), ())),
        precision=lax.Precision.HIGHEST,
        preferred_element_type=F32,
    )
    row = lax.broadcasted_iota(jnp.int32, (rank, rank), 0)
    col = lax.broadcasted_iota(jnp.int32, (rank, rank), 1)
    eye = row == col
    work = jnp.concatenate([gram, jnp.where(eye, 1.0, 0.0)], axis=1)
    below = lax.broadcasted_iota(jnp.int32, (rank, 1), 0)
    for j in range(rank - 1):
        pivot_row = work[j : j + 1, :]
        pivot_row = pivot_row / work[j : j + 1, j : j + 1]
        multiplier = jnp.where(below > j, work[:, j : j + 1], 0.0)
        work = work - multiplier * pivot_row
    diagonal = jnp.sum(jnp.where(eye, work[:, :rank], 0.0), axis=1, keepdims=True)
    inverse = work[:, rank:] / jnp.sqrt(diagonal)
    inverse_ref[...] = inverse
    rows = lax.dot_general(
        inverse,
        whole,
        (((1,), (0,)), ((), ())),
        precision=lax.Precision.HIGHEST,
        preferred_element_type=F32,
    )
    factor_ref[...] = (scale * rows).T


def finish_kernel(scale, q_ref, inverse_ref, out_ref):
    groups = q_ref.shape[0]
    raw = jnp.concatenate([q_ref[i] for i in range(groups)], axis=0)
    high, middle, low = parts_of(raw)
    inv_high, inv_middle, inv_low = parts_of(inverse_ref[...])
    left = jnp.concatenate([inv_high, inv_middle, inv_high, inv_high], axis=1)
    right = jnp.concatenate([high, high, middle, low], axis=0)
    whole = scale * dot(left, right, ((1,), (0,)))
    cin = out_ref.shape[2]
    for k in range(out_ref.shape[0]):
        out_ref[k] = whole[:, cin * k : cin * (k + 1)]


def solution(mesh):
    sizes = {"x": 4, "far": 4, "middle": 2, "near": 2, "y": 4, "c": 2}
    grid = Mesh(mesh.devices.reshape(tuple(sizes.values())), tuple(sizes))

    def count(axes):
        return math.prod(sizes[axis] for axis in axes)

    sample, channel = ("x", "far", "middle", "near"), ("y", "c")
    p_split, p_rest = ("x", "near", "y", "c"), ("far", "middle")
    q_split, q_rest = ("x", "middle", "near"), ("far",)

    p_first, far_first = {"x": 2, "y": 2, "near": 1}, {"far": 2, "middle": 1}
    q_first, last_first = {"x": 2, "middle": 1}, {"far": 2}

    def call(kernel, out_shape, in_specs, scratch, flops, moved, grant=40):
        return pl.pallas_call(
            kernel,
            out_shape=out_shape,
            in_specs=in_specs,
            out_specs=jax.tree.map(lambda _: VMEM, out_shape),
            scratch_shapes=scratch,
            compiler_params=pltpu.CompilerParams(vmem_limit_bytes=grant * 2**20),
            cost_estimate=pl.CostEstimate(flops=flops, bytes_accessed=moved, transcendentals=0),
        )

    def groups_of(axes, first):
        others = [axis for axis in sizes if axis not in axes]
        groups = []
        for place in itertools.product(*(range(sizes[axis]) for axis in others)):
            group = []
            for steps in itertools.product(*(range(sizes[axis]) for axis in axes)):
                at = dict(zip(others, place))
                for axis, step in zip(axes, steps):
                    at[axis] = (step + first.get(axis, 0)) % sizes[axis]
                index = 0
                for axis, size in sizes.items():
                    index = index * size + at[axis]
                group.append(index)
            groups.append(group)
        return groups

    def exchange(blocks, axes, first):
        if any(axis in first for axis in axes):
            return lax.all_to_all(
                blocks, tuple(sizes), 0, 0, tiled=True, axis_index_groups=groups_of(axes, first)
            )
        return lax.all_to_all(blocks, axes, 0, 0, tiled=True)

    def to_all(block, axes, first):
        return exchange(jnp.broadcast_to(block[None], (count(axes),) + block.shape), axes, first)

    def body(latent_in, out_grad, q_prev):
        rows, width, cout = out_grad.shape[1:]
        taps, cin, rank = q_prev.shape
        pixels = rows * width
        x = latent_in.reshape(-1, cin)
        g = out_grad.reshape(pixels, cout)
        q_turned = jnp.swapaxes(q_prev, 1, 2)
        whole_p = pltpu.VMEM((rank, cout), F32)

        p_term, x_held, g_held = call(
            lambda *refs: left_kernel(width, *refs),
            (
                jax.ShapeDtypeStruct((count(p_split), rank // count(p_split), cout), F32),
                jax.ShapeDtypeStruct(x.shape, BF16),
                jax.ShapeDtypeStruct(g.shape, BF16),
            ),
            [HBM, HBM, HBM],
            [pltpu.VMEM(q_turned.shape, BF16), pltpu.SemaphoreType.DMA((3,))],
            2 * pixels * cout * 256,
            2 * pixels * cout,
            grant=16,
        )(*(pltpu.with_memory_space_constraint(array, pltpu.HBM) for array in (x, q_turned, g)))
        piece = jnp.sum(exchange(p_term, p_split, p_first), axis=0)
        piece = jnp.sum(to_all(piece, p_rest, far_first), axis=0)
        p_pieces = to_all(piece, p_split, p_first)

        q_term = call(
            lambda *refs: right_kernel(width, *refs),
            jax.ShapeDtypeStruct((count(q_split), rank // count(q_split), taps * cin), F32),
            [VMEM, VMEM, VMEM],
            [whole_p],
            4 * pixels * cout * 256,
            2 * pixels * cout,
        )(p_pieces, x_held, g_held)

        part = jnp.sum(exchange(q_term, q_split, q_first), axis=0)
        inverse, p_whole = call(
            lambda *refs: factor_kernel(math.sqrt(cout), *refs),
            (jax.ShapeDtypeStruct((rank, rank), F32), jax.ShapeDtypeStruct((cout, rank), F32)),
            [VMEM],
            [whole_p],
            2 * pixels * cout * 256,
            2 * pixels * cout,
        )(p_pieces)
        share = cout // count(sample)
        at = lax.axis_index(sample) * share
        p_factor = lax.dynamic_slice_in_dim(p_whole, at, share, axis=0)
        part, inverse, p_factor = lax.optimization_barrier((part, inverse, p_factor))
        part = jnp.sum(to_all(part, q_rest, last_first), axis=0)
        q_raw = to_all(part, q_split, q_first)

        q_factor = call(
            lambda *refs: finish_kernel(1.0 / math.sqrt(cout), *refs),
            jax.ShapeDtypeStruct((taps, rank, cin), F32),
            [VMEM, VMEM],
            [],
            2 * taps * cin * rank * 256,
            8 * taps * cin * rank,
        )(q_raw, inverse)
        return p_factor, jnp.swapaxes(q_factor, 1, 2)

    return jax.shard_map(
        body,
        mesh=grid,
        in_specs=(P(sample, None, None, channel), P(sample, None, None, None), P(None, channel, None)),
        out_specs=(P(sample, None), P(None, channel, None)),
        check_vma=False,
    )
```

```python
import itertools
import math

import jax
import jax.numpy as jnp
from jax import lax
from jax.experimental import pallas as pl
from jax.experimental.pallas import tpu as pltpu
from jax.sharding import Mesh
from jax.sharding import PartitionSpec as P

F32 = jnp.float32
BF16 = jnp.bfloat16
VMEM = pl.BlockSpec(memory_space=pltpu.VMEM)
HBM = pl.BlockSpec(memory_space=pltpu.HBM)


def parts_of(value):
    high = value.astype(BF16)
    rest = value - high.astype(F32)
    middle = rest.astype(BF16)
    low = (rest - middle.astype(F32)).astype(BF16)
    return high, middle, low


def dot(left, right, dims):
    return lax.dot_general(left, right, (dims, ((), ())), preferred_element_type=F32)


def left_kernel(width, x_hbm, q_hbm, g_hbm, out_ref, x_ref, g_ref, q_ref, sems):
    loads = [
        pltpu.make_async_copy(source, target, sems.at[i])
        for i, (source, target) in enumerate(((x_hbm, x_ref), (q_hbm, q_ref), (g_hbm, g_ref)))
    ]
    for load in loads:
        load.start()
    loads[0].wait()
    loads[1].wait()
    pixels, rank, cin = g_ref.shape[0], q_ref.shape[1], q_ref.shape[2]
    taps = None
    for a in range(3):
        basis = q_ref[3 * a : 3 * a + 3].reshape(3 * rank, cin)
        term = dot(basis, x_ref[width * a : width * a + pixels, :], ((1,), (1,)))
        taps = term if taps is None else taps + term
    column = lax.broadcasted_iota(jnp.int32, (rank, pixels), 1) & (width - 1)
    before = pltpu.roll(taps[:rank], 1, 1)
    after = pltpu.roll(taps[2 * rank :], pixels - 1, 1)
    projected = (
        taps[rank : 2 * rank]
        + jnp.where(column == 0, 0.0, before)
        + jnp.where(column == width - 1, 0.0, after)
    )
    stacked = jnp.concatenate(parts_of(projected)[:2], axis=0)
    loads[2].wait()
    total = dot(stacked, g_ref[...], ((1,), (0,)))
    total = total[:rank] + total[rank:]
    rows = out_ref.shape[1]
    for i in range(out_ref.shape[0]):
        out_ref[i] = total[rows * i : rows * (i + 1)]


def gather_rows(pieces_ref, whole_ref):
    rows = pieces_ref.shape[1]
    for i in range(pieces_ref.shape[0]):
        whole_ref[rows * i : rows * (i + 1), :] = pieces_ref[i]


def right_kernel(width, p_ref, x_ref, g_ref, out_ref, whole_ref):
    gather_rows(p_ref, whole_ref)
    rank, pixels = whole_ref.shape[0], g_ref.shape[0]
    stacked = jnp.concatenate(parts_of(whole_ref[...])[:2], axis=0)
    mapped = dot(stacked, g_ref[...], ((1,), (1,)))
    mapped = mapped[:rank] + mapped[rank:]
    column = lax.broadcasted_iota(jnp.int32, (rank, pixels), 1) & (width - 1)
    ahead = jnp.where(column == width - 1, 0.0, pltpu.roll(mapped, pixels - 1, 1))
    behind = jnp.where(column == 0, 0.0, pltpu.roll(mapped, 1, 1))
    shifted = jnp.concatenate(
        [part for side in (ahead, mapped, behind) for part in parts_of(side)[:2]], axis=0
    )
    pieces = []
    for a in range(3):
        term = dot(shifted, x_ref[width * a : width * a + pixels, :], ((1,), (0,)))
        for b in range(3):
            t = term[2 * rank * b : 2 * rank * (b + 1)]
            pieces.append(t[:rank] + t[rank:])
    whole = jnp.concatenate(pieces, axis=1)
    groups, rows = out_ref.shape[0], out_ref.shape[1]
    for i in range(groups):
        out_ref[i] = whole[rows * i : rows * (i + 1)]


def factor_kernel(scale, p_ref, inverse_ref, factor_ref, whole_ref):
    gather_rows(p_ref, whole_ref)
    whole = whole_ref[...]
    rank = whole.shape[0]
    gram = lax.dot_general(
        whole,
        whole,
        (((1,), (1,)), ((), ())),
        precision=lax.Precision.HIGHEST,
        preferred_element_type=F32,
    )
    row = lax.broadcasted_iota(jnp.int32, (rank, rank), 0)
    col = lax.broadcasted_iota(jnp.int32, (rank, rank), 1)
    eye = row == col
    work = jnp.concatenate([gram, jnp.where(eye, 1.0, 0.0)], axis=1)
    below = lax.broadcasted_iota(jnp.int32, (rank, 1), 0)
    for j in range(rank - 1):
        pivot_row = work[j : j + 1, :]
        pivot_row = pivot_row / work[j : j + 1, j : j + 1]
        multiplier = jnp.where(below > j, work[:, j : j + 1], 0.0)
        work = work - multiplier * pivot_row
    diagonal = jnp.sum(jnp.where(eye, work[:, :rank], 0.0), axis=1, keepdims=True)
    inverse = work[:, rank:] / jnp.sqrt(diagonal)
    inverse_ref[...] = inverse
    rows = lax.dot_general(
        inverse,
        whole,
        (((1,), (0,)), ((), ())),
        precision=lax.Precision.HIGHEST,
        preferred_element_type=F32,
    )
    factor_ref[...] = (scale * rows).T


def finish_kernel(scale, q_ref, inverse_ref, out_ref):
    groups = q_ref.shape[0]
    raw = jnp.concatenate([q_ref[i] for i in range(groups)], axis=0)
    high, middle, low = parts_of(raw)
    inv_high, inv_middle, inv_low = parts_of(inverse_ref[...])
    left = jnp.concatenate([inv_high, inv_middle, inv_high, inv_high], axis=1)
    right = jnp.concatenate([high, high, middle, low], axis=0)
    whole = scale * dot(left, right, ((1,), (0,)))
    cin = out_ref.shape[2]
    for k in range(out_ref.shape[0]):
        out_ref[k] = whole[:, cin * k : cin * (k + 1)]


def solution(mesh):
    sizes = {"x": 4, "far": 4, "middle": 2, "near": 2, "y": 4, "c": 2}
    grid = Mesh(mesh.devices.reshape(tuple(sizes.values())), tuple(sizes))

    def count(axes):
        return math.prod(sizes[axis] for axis in axes)

    sample, channel = ("x", "far", "middle", "near"), ("y", "c")
    p_split, p_rest = ("x", "near", "y", "c"), ("far", "middle")
    q_split, q_rest = ("x", "middle", "near"), ("far",)

    p_first, far_first = {"x": 3, "y": 3, "near": 1}, {"far": 2, "middle": 1}
    q_first, last_first = {"x": 2, "middle": 1}, {"far": 2}

    def call(kernel, out_shape, in_specs, scratch, flops, moved, grant=40):
        return pl.pallas_call(
            kernel,
            out_shape=out_shape,
            in_specs=in_specs,
            out_specs=jax.tree.map(lambda _: VMEM, out_shape),
            scratch_shapes=scratch,
            compiler_params=pltpu.CompilerParams(vmem_limit_bytes=grant * 2**20),
            cost_estimate=pl.CostEstimate(flops=flops, bytes_accessed=moved, transcendentals=0),
        )

    def groups_of(axes, first):
        others = [axis for axis in sizes if axis not in axes]
        groups = []
        for place in itertools.product(*(range(sizes[axis]) for axis in others)):
            group = []
            for steps in itertools.product(*(range(sizes[axis]) for axis in axes)):
                at = dict(zip(others, place))
                for axis, step in zip(axes, steps):
                    at[axis] = (step + first.get(axis, 0)) % sizes[axis]
                index = 0
                for axis, size in sizes.items():
                    index = index * size + at[axis]
                group.append(index)
            groups.append(group)
        return groups

    def exchange(blocks, axes, first):
        if any(axis in first for axis in axes):
            return lax.all_to_all(
                blocks, tuple(sizes), 0, 0, tiled=True, axis_index_groups=groups_of(axes, first)
            )
        return lax.all_to_all(blocks, axes, 0, 0, tiled=True)

    def to_all(block, axes, first):
        return exchange(jnp.broadcast_to(block[None], (count(axes),) + block.shape), axes, first)

    def body(latent_in, out_grad, q_prev):
        rows, width, cout = out_grad.shape[1:]
        taps, cin, rank = q_prev.shape
        pixels = rows * width
        x = latent_in.reshape(-1, cin)
        g = out_grad.reshape(pixels, cout)
        q_turned = jnp.swapaxes(q_prev, 1, 2)
        whole_p = pltpu.VMEM((rank, cout), F32)

        p_term, x_held, g_held = call(
            lambda *refs: left_kernel(width, *refs),
            (
                jax.ShapeDtypeStruct((count(p_split), rank // count(p_split), cout), F32),
                jax.ShapeDtypeStruct(x.shape, BF16),
                jax.ShapeDtypeStruct(g.shape, BF16),
            ),
            [HBM, HBM, HBM],
            [pltpu.VMEM(q_turned.shape, BF16), pltpu.SemaphoreType.DMA((3,))],
            2 * pixels * cout * 256,
            2 * pixels * cout,
            grant=16,
        )(*(pltpu.with_memory_space_constraint(array, pltpu.HBM) for array in (x, q_turned, g)))
        piece = jnp.sum(exchange(p_term, p_split, p_first), axis=0)
        piece = jnp.sum(to_all(piece, p_rest, far_first), axis=0)
        p_pieces = to_all(piece, p_split, p_first)

        q_term = call(
            lambda *refs: right_kernel(width, *refs),
            jax.ShapeDtypeStruct((count(q_split), rank // count(q_split), taps * cin), F32),
            [VMEM, VMEM, VMEM],
            [whole_p],
            4 * pixels * cout * 256,
            2 * pixels * cout,
        )(p_pieces, x_held, g_held)

        part = jnp.sum(exchange(q_term, q_split, q_first), axis=0)
        inverse, p_whole = call(
            lambda *refs: factor_kernel(math.sqrt(cout), *refs),
            (jax.ShapeDtypeStruct((rank, rank), F32), jax.ShapeDtypeStruct((cout, rank), F32)),
            [VMEM],
            [whole_p],
            2 * pixels * cout * 256,
            2 * pixels * cout,
        )(p_pieces)
        share = cout // count(sample)
        at = lax.axis_index(sample) * share
        p_factor = lax.dynamic_slice_in_dim(p_whole, at, share, axis=0)
        part, inverse, p_factor = lax.optimization_barrier((part, inverse, p_factor))
        part = jnp.sum(to_all(part, q_rest, last_first), axis=0)
        q_raw = to_all(part, q_split, q_first)

        q_factor = call(
            lambda *refs: finish_kernel(1.0 / math.sqrt(cout), *refs),
            jax.ShapeDtypeStruct((taps, rank, cin), F32),
            [VMEM, VMEM],
            [],
            2 * taps * cin * rank * 256,
            8 * taps * cin * rank,
        )(q_raw, inverse)
        return p_factor, jnp.swapaxes(q_factor, 1, 2)

    return jax.shard_map(
        body,
        mesh=grid,
        in_specs=(P(sample, None, None, channel), P(sample, None, None, None), P(None, channel, None)),
        out_specs=(P(sample, None), P(None, channel, None)),
        check_vma=False,
    )
```

```python
import itertools
import math

import jax
import jax.numpy as jnp
from jax import lax
from jax.experimental import pallas as pl
from jax.experimental.pallas import tpu as pltpu
from jax.sharding import Mesh
from jax.sharding import PartitionSpec as P

F32 = jnp.float32
BF16 = jnp.bfloat16
VMEM = pl.BlockSpec(memory_space=pltpu.VMEM)
HBM = pl.BlockSpec(memory_space=pltpu.HBM)


def parts_of(value):
    high = value.astype(BF16)
    rest = value - high.astype(F32)
    middle = rest.astype(BF16)
    low = (rest - middle.astype(F32)).astype(BF16)
    return high, middle, low


def dot(left, right, dims):
    return lax.dot_general(left, right, (dims, ((), ())), preferred_element_type=F32)


def left_kernel(width, x_hbm, q_hbm, g_hbm, out_ref, x_ref, g_ref, q_ref, sems):
    loads = [
        pltpu.make_async_copy(source, target, sems.at[i])
        for i, (source, target) in enumerate(((x_hbm, x_ref), (q_hbm, q_ref), (g_hbm, g_ref)))
    ]
    for load in loads:
        load.start()
    loads[0].wait()
    loads[1].wait()
    pixels, rank, cin = g_ref.shape[0], q_ref.shape[1], q_ref.shape[2]
    taps = None
    for a in range(3):
        basis = q_ref[3 * a : 3 * a + 3].reshape(3 * rank, cin)
        term = dot(basis, x_ref[width * a : width * a + pixels, :], ((1,), (1,)))
        taps = term if taps is None else taps + term
    column = lax.broadcasted_iota(jnp.int32, (rank, pixels), 1) & (width - 1)
    before = pltpu.roll(taps[:rank], 1, 1)
    after = pltpu.roll(taps[2 * rank :], pixels - 1, 1)
    projected = (
        taps[rank : 2 * rank]
        + jnp.where(column == 0, 0.0, before)
        + jnp.where(column == width - 1, 0.0, after)
    )
    stacked = jnp.concatenate(parts_of(projected)[:2], axis=0)
    loads[2].wait()
    total = dot(stacked, g_ref[...], ((1,), (0,)))
    total = total[:rank] + total[rank:]
    rows = out_ref.shape[1]
    for i in range(out_ref.shape[0]):
        out_ref[i] = total[rows * i : rows * (i + 1)]


def gather_rows(pieces_ref, whole_ref):
    rows = pieces_ref.shape[1]
    for i in range(pieces_ref.shape[0]):
        whole_ref[rows * i : rows * (i + 1), :] = pieces_ref[i]


def right_kernel(width, p_ref, x_ref, g_ref, out_ref, whole_ref):
    gather_rows(p_ref, whole_ref)
    rank, pixels = whole_ref.shape[0], g_ref.shape[0]
    stacked = jnp.concatenate(parts_of(whole_ref[...])[:2], axis=0)
    mapped = dot(stacked, g_ref[...], ((1,), (1,)))
    mapped = mapped[:rank] + mapped[rank:]
    column = lax.broadcasted_iota(jnp.int32, (rank, pixels), 1) & (width - 1)
    ahead = jnp.where(column == width - 1, 0.0, pltpu.roll(mapped, pixels - 1, 1))
    behind = jnp.where(column == 0, 0.0, pltpu.roll(mapped, 1, 1))
    shifted = jnp.concatenate(
        [part for side in (ahead, mapped, behind) for part in parts_of(side)[:2]], axis=0
    )
    pieces = []
    for a in range(3):
        term = dot(shifted, x_ref[width * a : width * a + pixels, :], ((1,), (0,)))
        for b in range(3):
            t = term[2 * rank * b : 2 * rank * (b + 1)]
            pieces.append(t[:rank] + t[rank:])
    whole = jnp.concatenate(pieces, axis=1)
    groups, rows = out_ref.shape[0], out_ref.shape[1]
    for i in range(groups):
        out_ref[i] = whole[rows * i : rows * (i + 1)]


def factor_kernel(scale, p_ref, inverse_ref, factor_ref, whole_ref):
    gather_rows(p_ref, whole_ref)
    whole = whole_ref[...]
    rank = whole.shape[0]
    gram = lax.dot_general(
        whole,
        whole,
        (((1,), (1,)), ((), ())),
        precision=lax.Precision.HIGHEST,
        preferred_element_type=F32,
    )
    row = lax.broadcasted_iota(jnp.int32, (rank, rank), 0)
    col = lax.broadcasted_iota(jnp.int32, (rank, rank), 1)
    eye = row == col
    work = jnp.concatenate([gram, jnp.where(eye, 1.0, 0.0)], axis=1)
    below = lax.broadcasted_iota(jnp.int32, (rank, 1), 0)
    for j in range(rank - 1):
        pivot_row = work[j : j + 1, :]
        pivot_row = pivot_row / work[j : j + 1, j : j + 1]
        multiplier = jnp.where(below > j, work[:, j : j + 1], 0.0)
        work = work - multiplier * pivot_row
    diagonal = jnp.sum(jnp.where(eye, work[:, :rank], 0.0), axis=1, keepdims=True)
    inverse = work[:, rank:] / jnp.sqrt(diagonal)
    inverse_ref[...] = inverse
    rows = lax.dot_general(
        inverse,
        whole,
        (((1,), (0,)), ((), ())),
        precision=lax.Precision.HIGHEST,
        preferred_element_type=F32,
    )
    factor_ref[...] = (scale * rows).T


def finish_kernel(scale, q_ref, inverse_ref, out_hbm, taps_ref, sems):
    groups = q_ref.shape[0]
    raw = jnp.concatenate([q_ref[i] for i in range(groups)], axis=0)
    high, middle, low = parts_of(raw)
    inv_high, inv_middle, inv_low = parts_of(scale * inverse_ref[...])
    left = jnp.concatenate([inv_high, inv_middle, inv_high, inv_high], axis=1)
    right = jnp.concatenate([high, high, middle, low], axis=0)
    whole = dot(left, right, ((1,), (0,)))
    cin = taps_ref.shape[2]
    stores = []
    for k in range(taps_ref.shape[0]):
        taps_ref[k] = whole[:, cin * k : cin * (k + 1)]
        stores.append(pltpu.make_async_copy(taps_ref.at[k], out_hbm.at[k], sems.at[k]))
        stores[-1].start()
    for store in stores:
        store.wait()


def solution(mesh):
    sizes = {"x": 4, "far": 4, "middle": 2, "near": 2, "y": 4, "c": 2}
    grid = Mesh(mesh.devices.reshape(tuple(sizes.values())), tuple(sizes))

    def count(axes):
        return math.prod(sizes[axis] for axis in axes)

    sample, channel = ("x", "far", "middle", "near"), ("y", "c")
    p_split, p_rest = ("x", "near", "y", "c"), ("far", "middle")
    q_split, q_rest = ("x", "middle", "near"), ("far",)

    p_first, far_first = {"x": 3, "y": 3, "near": 1}, {"far": 2, "middle": 1}
    q_first, last_first = {"x": 2, "middle": 1}, {"far": 2}

    def call(kernel, out_shape, in_specs, scratch, flops, moved, grant=40, out=VMEM):
        return pl.pallas_call(
            kernel,
            out_shape=out_shape,
            in_specs=in_specs,
            out_specs=jax.tree.map(lambda _: out, out_shape),
            scratch_shapes=scratch,
            compiler_params=pltpu.CompilerParams(vmem_limit_bytes=grant * 2**20),
            cost_estimate=pl.CostEstimate(flops=flops, bytes_accessed=moved, transcendentals=0),
        )

    def groups_of(axes, first):
        others = [axis for axis in sizes if axis not in axes]
        groups = []
        for place in itertools.product(*(range(sizes[axis]) for axis in others)):
            group = []
            for steps in itertools.product(*(range(sizes[axis]) for axis in axes)):
                at = dict(zip(others, place))
                for axis, step in zip(axes, steps):
                    at[axis] = (step + first.get(axis, 0)) % sizes[axis]
                index = 0
                for axis, size in sizes.items():
                    index = index * size + at[axis]
                group.append(index)
            groups.append(group)
        return groups

    def exchange(blocks, axes, first):
        if any(axis in first for axis in axes):
            return lax.all_to_all(
                blocks, tuple(sizes), 0, 0, tiled=True, axis_index_groups=groups_of(axes, first)
            )
        return lax.all_to_all(blocks, axes, 0, 0, tiled=True)

    def to_all(block, axes, first):
        return exchange(jnp.broadcast_to(block[None], (count(axes),) + block.shape), axes, first)

    def body(latent_in, out_grad, q_prev):
        rows, width, cout = out_grad.shape[1:]
        taps, cin, rank = q_prev.shape
        pixels = rows * width
        x = latent_in.reshape(-1, cin)
        g = out_grad.reshape(pixels, cout)
        q_turned = jnp.swapaxes(q_prev, 1, 2)
        whole_p = pltpu.VMEM((rank, cout), F32)

        p_term, x_held, g_held = call(
            lambda *refs: left_kernel(width, *refs),
            (
                jax.ShapeDtypeStruct((count(p_split), rank // count(p_split), cout), F32),
                jax.ShapeDtypeStruct(x.shape, BF16),
                jax.ShapeDtypeStruct(g.shape, BF16),
            ),
            [HBM, HBM, HBM],
            [pltpu.VMEM(q_turned.shape, BF16), pltpu.SemaphoreType.DMA((3,))],
            2 * pixels * cout * 256,
            2 * pixels * cout,
            grant=16,
        )(*(pltpu.with_memory_space_constraint(array, pltpu.HBM) for array in (x, q_turned, g)))
        piece = jnp.sum(exchange(p_term, p_split, p_first), axis=0)
        piece = jnp.sum(to_all(piece, p_rest, far_first), axis=0)
        p_pieces = to_all(piece, p_split, p_first)

        q_term = call(
            lambda *refs: right_kernel(width, *refs),
            jax.ShapeDtypeStruct((count(q_split), rank // count(q_split), taps * cin), F32),
            [VMEM, VMEM, VMEM],
            [whole_p],
            4 * pixels * cout * 256,
            2 * pixels * cout,
        )(p_pieces, x_held, g_held)

        part = jnp.sum(exchange(q_term, q_split, q_first), axis=0)
        inverse, p_whole = call(
            lambda *refs: factor_kernel(math.sqrt(cout), *refs),
            (jax.ShapeDtypeStruct((rank, rank), F32), jax.ShapeDtypeStruct((cout, rank), F32)),
            [VMEM],
            [whole_p],
            2 * pixels * cout * 256,
            2 * pixels * cout,
        )(p_pieces)
        share = cout // count(sample)
        at = lax.axis_index(sample) * share
        p_factor = lax.dynamic_slice_in_dim(p_whole, at, share, axis=0)
        part, inverse, p_factor = lax.optimization_barrier((part, inverse, p_factor))
        part = jnp.sum(to_all(part, q_rest, last_first), axis=0)
        q_raw = to_all(part, q_split, q_first)

        q_factor = call(
            lambda *refs: finish_kernel(1.0 / math.sqrt(cout), *refs),
            jax.ShapeDtypeStruct((taps, rank, cin), F32),
            [VMEM, VMEM],
            [pltpu.VMEM((taps, rank, cin), F32), pltpu.SemaphoreType.DMA((taps,))],
            2 * taps * cin * rank * 256,
            8 * taps * cin * rank,
            out=HBM,
        )(q_raw, inverse)
        return p_factor, jnp.swapaxes(q_factor, 1, 2)

    return jax.shard_map(
        body,
        mesh=grid,
        in_specs=(P(sample, None, None, channel), P(sample, None, None, None), P(None, channel, None)),
        out_specs=(P(sample, None), P(None, channel, None)),
        check_vma=False,
    )
```
